512 devices in a mesh: frame: 16 (over x, y_hi, core), patch: 32 (over y_lo, z).
Axes of the slice: x: 4, y: 8 (y_hi: 2, y_lo: 4; y = y_hi * 4 + y_lo), z: 8, core: 2. Of those that a mesh axis runs over, the one named last changes fastest.
Arguments:
- features: bfloat16 [64, 32, 128, 320], P('frame', 'patch'), may hold values from -6 to 6
- stale_edges: bfloat16 [64, 64, 128, 320], P('frame', 'patch'), may hold values from -6 to 6
- conv_weight: bfloat16 [3, 3, 320, 320], P(None, None, None, 'frame'), may hold values from -0.109375 to 0.109375
- conv_bias: float32 [320], replicated, may hold values from -3 to 3
- first_gain: float32 [320], replicated, may hold values from 0.1 to 1.9
- first_shift: float32 [320], replicated, may hold values from -2 to 2
- query_weight: bfloat16 [320, 320], replicated, may hold values from -4 to 4
- key_weight: bfloat16 [320, 320], replicated, may hold values from -4 to 4
- value_weight: bfloat16 [320, 320], replicated, may hold values from -0.3125 to 0.3125
- out_weight: bfloat16 [320, 320], replicated, may hold values from -0.3125 to 0.3125
- out_bias: float32 [320], replicated, may hold values from -2 to 2
- second_gain: float32 [320], replicated, may hold values from 0.1 to 1.9
- second_shift: float32 [320], replicated, may hold values from -2 to 2
- geglu_weight: bfloat16 [320, 2560], replicated, may hold values from -0.3125 to 0.3125
- geglu_bias: float32 [2560], replicated, may hold values from -2 to 2
- down_weight: bfloat16 [1280, 320], replicated, may hold values from -0.15625 to 0.15625
- down_bias: float32 [320], replicated, may hold values from -2 to 2
Outputs:
- block_out: bfloat16 [64, 32, 128, 320], P('frame', 'patch')
The draws below stay inside these ranges and needn't reach their ends.
All inputs are finite; a program needn't handle non-finite values.
Results may differ from the reference program's by a relative error of at most 0.02.
Values may be sent and summed in bfloat16 or wider, within the bound.
No kernel may reach another device: no remote copies, remote signals or barrier semaphores. Data moves between devices by JAX's collectives and lax.ppermute only.
A program may use at most 64 MiB of HBM per device.

```python
import math
import jax
import jax.numpy as jnp
from jax import lax

CH = 320
HEADS = 8
FF = 1280
R_DEV = 1
COLS = 128
FRAMES = 64
BANDS = 32
ROWS = 32


def draw_query_weight(key, part):
    key = jax.random.fold_in(key, 5)
    private = jax.random.normal(key, (CH, CH), jnp.float32) / math.sqrt(CH)
    matrix = private
    return jnp.clip(matrix, -4.0, 4.0).astype(jnp.bfloat16)


def draw_key_weight(key, part):
    key = jax.random.fold_in(key, 7)
    private = jax.random.normal(key, (CH, CH), jnp.float32) / math.sqrt(CH)
    matrix = private
    return jnp.clip(matrix, -4.0, 4.0).astype(jnp.bfloat16)


def level_of(own_key, dims, shards, least, high):
    def one(dim, parts):
        draws = jax.random.uniform(jax.random.fold_in(jax.random.fold_in(own_key, 6), dim), (parts,), jnp.float32, least / len(shards), high / len(shards))
        return jnp.repeat(jnp.exp(draws), dims[dim] // parts).reshape((-1,) + (1,) * (len(dims) - dim - 1))

    level = one(*shards[0])
    for cut in shards[1:]:
        level = level * one(*cut)
    return level


def bell_draw(own_key, shape, spread, bound, shards=(), kind=jnp.bfloat16):
    entries = jax.random.normal(own_key, shape, jnp.float32) * spread
    if len(shards) > 0:
        entries = level_of(own_key, shape, shards, -0.22, 0.18) * entries
    return jnp.clip(entries, min=-bound, max=bound).astype(kind)


def setup_inputs(seed: int = 0) -> dict:
    seeds = jax.random.split(jax.random.key(seed), 18)
    features = bell_draw(seeds[0], (FRAMES, ROWS, COLS, CH), 1.0, 6.0, ((0, 16), (1, 32)))
    stale_edges = bell_draw(seeds[1], (FRAMES, 2 * BANDS, COLS, CH), 1.0, 6.0, ((0, 16), (1, 32)))
    conv_weight = bell_draw(seeds[2], (3, 3, CH, CH), (9 * CH) ** -0.5, 0.109375, ((3, 16),))
    conv_bias = bell_draw(seeds[3], (CH,), 0.5, 3.0, (), jnp.float32)
    first_gain = jnp.clip(1.0 + 0.18 * jax.random.normal(seeds[4], (CH,), jnp.float32), 0.1, 1.9)
    first_shift = bell_draw(seeds[5], (CH,), 0.3, 2.0, (), jnp.float32)
    query_weight = draw_query_weight(jax.random.fold_in(seeds[17], 71), 0)
    key_weight = draw_key_weight(jax.random.fold_in(seeds[17], 71), 0)
    value_weight = bell_draw(seeds[8], (CH, CH), CH ** -0.5, 0.3125)
    out_weight = bell_draw(seeds[9], (CH, CH), CH ** -0.5, 0.3125)
    out_bias = bell_draw(seeds[10], (CH,), 0.3, 2.0, (), jnp.float32)
    second_gain = jnp.clip(1.0 + 0.18 * jax.random.normal(seeds[11], (CH,), jnp.float32), 0.1, 1.9)
    second_shift = bell_draw(seeds[12], (CH,), 0.3, 2.0, (), jnp.float32)
    geglu_weight = bell_draw(seeds[13], (CH, 2 * FF), CH ** -0.5, 0.3125)
    geglu_bias = bell_draw(seeds[14], (2 * FF,), 0.3, 2.0, (), jnp.float32)
    down_weight = bell_draw(seeds[15], (FF, CH), FF ** -0.5, 0.15625)
    down_bias = bell_draw(seeds[16], (CH,), 0.3, 2.0, (), jnp.float32)
    return {"features": features, "stale_edges": stale_edges, "conv_weight": conv_weight, "conv_bias": conv_bias, "first_gain": first_gain, "first_shift": first_shift, "query_weight": query_weight, "key_weight": key_weight, "value_weight": value_weight, "out_weight": out_weight, "out_bias": out_bias, "second_gain": second_gain, "second_shift": second_shift, "geglu_weight": geglu_weight, "geglu_bias": geglu_bias, "down_weight": down_weight, "down_bias": down_bias}


def rounded(values):
    return lax.optimization_barrier(values.astype(jnp.bfloat16))

def layer_norm(inputs, gain_vec, shift_vec):
    average = lax.optimization_barrier(jnp.mean(inputs, axis=-1, keepdims=True))
    centred = inputs - average
    variance = lax.optimization_barrier(jnp.mean(centred * centred, axis=-1, keepdims=True))
    return centred * lax.rsqrt(variance + 1e-05) * gain_vec + shift_vec

def position_table(positions, channels):
    halves = jnp.arange(channels // 2).astype(positions.dtype)
    rates = jnp.exp(halves * (-2.0 * math.log(10000.0) / channels))
    angles = positions[:, None] * rates[None, :]
    return jnp.stack([jnp.sin(angles), jnp.cos(angles)], axis=-1).reshape(positions.shape[0], channels)

def attend(queries, key_rows, value_rows):
    frame_count, pixel_count, channels = queries.shape
    head_dim = channels // HEADS
    shaped = (frame_count, pixel_count, HEADS, head_dim)
    scores = jnp.einsum('fnhd,gnhd->nhfg', queries.reshape(shaped).astype(jnp.float32), key_rows.reshape(shaped).astype(jnp.float32)) / math.sqrt(head_dim)
    scores = scores - lax.optimization_barrier(jnp.max(scores, axis=-1, keepdims=True))
    expo_scores = jnp.exp(scores)
    attn_probs = rounded(expo_scores / lax.optimization_barrier(jnp.sum(expo_scores, axis=-1, keepdims=True)))
    context = jnp.einsum('nhfg,gnhd->fnhd', attn_probs.astype(jnp.float32), value_rows.reshape(shaped).astype(jnp.float32))
    return context.astype(jnp.bfloat16).reshape(frame_count, pixel_count, channels)

def reference(features, stale_edges, conv_weight, conv_bias, first_gain, first_shift, query_weight, key_weight, value_weight, out_weight, out_bias, second_gain, second_shift, geglu_weight, geglu_bias, down_weight, down_bias):

    def conv_frame(frame_pair):
        frame_rows, frame_edges = frame_pair
        bands = frame_rows.reshape(BANDS, R_DEV, COLS, CH)
        edges = frame_edges.reshape(BANDS, 2, COLS, CH)
        zero_row = jnp.zeros((1, COLS, CH), jnp.bfloat16)
        above = jnp.concatenate([zero_row, edges[:-1, 1]], axis=0)
        below = jnp.concatenate([edges[1:, 0], zero_row], axis=0)
        padded = jnp.concatenate([above[:, None], bands, below[:, None]], axis=1)
        padded = jnp.pad(padded, ((0, 0), (0, 0), (1, 1), (0, 0)))
        summed = jnp.zeros((BANDS * R_DEV * COLS, CH), jnp.float32)
        for row_step in range(3):
            for col_step in range(3):
                window = padded[:, row_step:row_step + R_DEV, col_step:col_step + COLS].reshape(-1, CH)
                summed = summed + jnp.dot(window, conv_weight[row_step, col_step], preferred_element_type=jnp.float32)
        return (summed + conv_bias).astype(jnp.bfloat16).reshape(ROWS, COLS, CH)
    conv_out = lax.map(conv_frame, (features, stale_edges))
    position = position_table(jnp.arange(FRAMES).astype(conv_bias.dtype), CH)

    def temporal(rows):
        flat = rows.reshape(-1, CH)
        normed = rounded(layer_norm(rows.astype(jnp.float32), first_gain, first_shift) + position[:, None, :])
        normed = normed.reshape(-1, CH)
        queries = rounded(jnp.dot(normed, query_weight, preferred_element_type=jnp.float32)).reshape(rows.shape)
        key_rows = rounded(jnp.dot(normed, key_weight, preferred_element_type=jnp.float32)).reshape(rows.shape)
        value_rows = rounded(jnp.dot(normed, value_weight, preferred_element_type=jnp.float32)).reshape(rows.shape)
        context = attend(queries, key_rows, value_rows).reshape(-1, CH)
        attn_out = rounded(jnp.dot(context, out_weight, preferred_element_type=jnp.float32) + out_bias)
        middle = rounded(flat.astype(jnp.float32) + attn_out.astype(jnp.float32))
        normed_two = rounded(layer_norm(middle.astype(jnp.float32), second_gain, second_shift))
        projected = jnp.dot(normed_two, geglu_weight, preferred_element_type=jnp.float32) + geglu_bias
        hidden = rounded(projected[:, :FF] * jax.nn.gelu(projected[:, FF:], approximate=False))
        output = middle.astype(jnp.float32) + jnp.dot(hidden, down_weight, preferred_element_type=jnp.float32) + down_bias
        return output.astype(jnp.bfloat16).reshape(rows.shape)
    by_rows = jnp.moveaxis(conv_out, 1, 0)
    result = lax.map(temporal, by_rows)
    return jnp.moveaxis(result, 0, 1)
```

```python
import functools
import math

import jax
import jax.numpy as jnp
import numpy as np
from jax import lax
from jax.experimental import pallas as pl
from jax.experimental.pallas import tpu as pltpu
from jax.sharding import Mesh, PartitionSpec as P

HEADS = 8
CH = 320
FF = 1280
TAPS_IN = 960
TAPS_PAD = 1024
SLOT = 24
SHARE = 20
FRAMES = 64
COLS = 128
PATCHES = 32
MIB = 1024 * 1024


def pack_weight_kernel(w_ref, out_ref):
    for b in range(3):
        rows = jnp.concatenate(
            [w_ref[a, b].astype(jnp.float32) for a in range(3)]
            + [jnp.zeros((SHARE, TAPS_PAD - TAPS_IN), jnp.float32)],
            axis=1,
        )
        rows = jnp.concatenate(
            [rows, jnp.zeros((SLOT - SHARE, TAPS_PAD), jnp.float32)], axis=0
        )
        out_ref[:, b * TAPS_PAD : (b + 1) * TAPS_PAD] = rows.astype(jnp.bfloat16)


def tokens_kernel(above_ref, band_ref, below_ref, out_ref):
    for f in range(4):
        stacked = jnp.concatenate(
            [above_ref[f], band_ref[f], below_ref[f], jnp.zeros((TAPS_PAD - TAPS_IN, COLS), jnp.bfloat16)],
            axis=0,
        )
        out_ref[f * COLS : (f + 1) * COLS, :] = stacked.T


def conv_kernel(x_ref, sibling_ref, w_ref, bias_ref, sel_ref, out_ref):
    x = jnp.concatenate([x_ref[...], sibling_ref[...]], axis=0)
    tokens = x.shape[0]
    position = lax.broadcasted_iota(jnp.int32, (tokens, 1), 0) % COLS

    def taps(b):
        weight = w_ref[:, :, b * TAPS_PAD : (b + 1) * TAPS_PAD].reshape(-1, TAPS_PAD)
        return lax.dot_general(
            x, weight, (((1,), (1,)), ((), ())), preferred_element_type=jnp.float32
        )

    left = jnp.where(position == 0, 0.0, pltpu.roll(taps(0), 1, 0))
    right = jnp.where(position == COLS - 1, 0.0, pltpu.roll(taps(2), tokens - 1, 0))
    summed = taps(1) + left + right + bias_ref[...]
    ordered = jnp.dot(
        summed.astype(jnp.bfloat16), sel_ref[...], preferred_element_type=jnp.float32
    )
    by_owner = ordered.reshape(2, 2, 2, 16, 8, CH // 2)
    for k in range(16):
        groups = [
            jnp.concatenate([by_owner[core, high, 0, k], by_owner[core, high, 1, k]], axis=0)
            for core in range(2)
            for high in range(2)
        ]
        out_ref[k] = jnp.concatenate(groups, axis=1).astype(jnp.bfloat16)


def norm_rows(values, gain, shift):
    average = jnp.mean(values, axis=-1, keepdims=True)
    centred = values - average
    variance = jnp.mean(centred * centred, axis=-1, keepdims=True)
    return centred * lax.rsqrt(variance + 1e-05) * gain + shift


def block_kernel(
    x_ref,
    order_ref,
    position_ref,
    first_gain_ref,
    first_shift_ref,
    query_ref,
    key_ref,
    value_ref,
    out_weight_ref,
    out_bias_ref,
    second_gain_ref,
    second_shift_ref,
    geglu_ref,
    geglu_bias_ref,
    down_ref,
    down_bias_ref,
    out_ref,
    rows_ref,
    context_ref,
):
    pixels = 8
    blocks = 2 * CH // 128
    half = CH // 2
    received = x_ref[...].astype(jnp.float32).reshape(8, 2, 16, 2 * CH)
    for core in range(2):
        for i in range(blocks):
            rows_ref[core, i] = received[:, core, :, i * 128 : (i + 1) * 128].reshape(128, 128)
    x = jnp.zeros((pixels * FRAMES, CH), jnp.float32)
    for core in range(2):
        pieces = []
        for p in range(pixels):
            row = jnp.concatenate(
                [rows_ref[core, i, pl.ds(p, 16, stride=pixels), :] for i in range(blocks)], axis=1
            )
            for owner_core in range(2):
                for high in range(2):
                    group = (owner_core ^ core) * 2 + high
                    pieces.append(row[:, group * half : (group + 1) * half])
        x += jnp.dot(
            jnp.concatenate(pieces, axis=0).astype(jnp.bfloat16),
            order_ref[core],
            preferred_element_type=jnp.float32,
        )
    position = position_ref[...]
    normed = norm_rows(x, first_gain_ref[...], first_shift_ref[...]).reshape(pixels, FRAMES, CH)
    normed = (normed + position[None]).reshape(pixels * FRAMES, CH).astype(jnp.bfloat16)

    def project(weight_ref):
        return jnp.dot(normed, weight_ref[...], preferred_element_type=jnp.float32).astype(
            jnp.bfloat16
        )

    queries, key_rows, value_rows = project(query_ref), project(key_ref), project(value_ref)
    head_dim = CH // HEADS
    channel = lax.broadcasted_iota(jnp.int32, (1, CH), 1)
    head_masks = [
        (channel >= h * head_dim) & (channel < (h + 1) * head_dim) for h in range(HEADS)
    ]
    for p in range(pixels):
        rows = slice(p * FRAMES, (p + 1) * FRAMES)
        query = queries[rows]
        stacked = jnp.concatenate(
            [jnp.where(m, query, jnp.zeros_like(query)) for m in head_masks], axis=0
        )
        scores = lax.dot_general(
            stacked, key_rows[rows], (((1,), (1,)), ((), ())), preferred_element_type=jnp.float32
        ) * (1.0 / math.sqrt(head_dim))
        expo = jnp.exp(scores - jnp.max(scores, axis=-1, keepdims=True))
        probs = (expo / jnp.sum(expo, axis=-1, keepdims=True)).astype(jnp.bfloat16)
        mixed = jnp.dot(probs, value_rows[rows], preferred_element_type=jnp.float32)
        context = jnp.zeros((FRAMES, CH), jnp.float32)
        for h in range(HEADS):
            context = jnp.where(head_masks[h], mixed[h * FRAMES : (h + 1) * FRAMES], context)
        context_ref[rows, :] = context.astype(jnp.bfloat16)
    attn_out = (
        jnp.dot(context_ref[...], out_weight_ref[...], preferred_element_type=jnp.float32)
        + out_bias_ref[...]
    ).astype(jnp.bfloat16)
    middle = (x + attn_out.astype(jnp.float32)).astype(jnp.bfloat16).astype(jnp.float32)
    normed_two = norm_rows(middle, second_gain_ref[...], second_shift_ref[...]).astype(jnp.bfloat16)
    total = middle + down_bias_ref[...]
    step = 256
    for start in range(0, FF, step):
        lanes = slice(start, start + step)
        gates = slice(FF + start, FF + start + step)
        value = (
            jnp.dot(normed_two, geglu_ref[:, lanes], preferred_element_type=jnp.float32)
            + geglu_bias_ref[:, lanes]
        )
        gate = (
            jnp.dot(normed_two, geglu_ref[:, gates], preferred_element_type=jnp.float32)
            + geglu_bias_ref[:, gates]
        )
        hidden = value * (0.5 * gate * (1.0 + lax.erf(gate * (1.0 / math.sqrt(2.0)))))
        total = total + jnp.dot(
            hidden.astype(jnp.bfloat16), down_ref[lanes, :], preferred_element_type=jnp.float32
        )
    for core in range(2):
        for p in range(pixels):
            start = p * FRAMES + core * 32
            both = jnp.concatenate([total[start : start + 16], total[start + 16 : start + 32]], axis=1)
            for i in range(blocks):
                rows_ref[core, i, pl.ds(p, 16, stride=pixels), :] = both[:, i * 128 : (i + 1) * 128]
        for i in range(blocks):
            out_ref[:, core, :, i * 128 : (i + 1) * 128] = (
                rows_ref[core, i].astype(jnp.bfloat16).reshape(8, 16, 128)
            )


def finish_kernel(x_ref, out_ref):
    received = x_ref[...].astype(jnp.float32)
    for half in range(2):
        lanes = slice(half * CH, (half + 1) * CH)
        for f in range(2):
            rows = received[:, f * 8 : (f + 1) * 8, lanes].reshape(COLS, CH)
            out_ref[half * 2 + f] = rows.T.astype(jnp.bfloat16)


def call(kernel, out_shape, flops, scratch=(), dtype=jnp.bfloat16):
    return pl.pallas_call(
        kernel,
        out_shape=jax.ShapeDtypeStruct(out_shape, dtype),
        scratch_shapes=list(scratch),
        compiler_params=pltpu.CompilerParams(vmem_limit_bytes=48 * MIB),
        cost_estimate=pl.CostEstimate(flops=flops, bytes_accessed=4 * MIB, transcendentals=0),
    )


def position_rows():
    frames = np.array(
        [
            (chip * 2 + core) * 4 + high * 2 + low
            for core in range(2)
            for high in range(2)
            for chip in range(8)
            for low in range(2)
        ]
    )
    rates = 10000.0 ** (-2.0 * np.arange(CH // 2) / CH)
    angles = frames[:, None] * rates[None, :]
    return np.stack([np.sin(angles), np.cos(angles)], axis=-1).reshape(FRAMES, CH).astype(np.float32)


def channel_order():
    order = np.zeros((2, CH // 2, CH), np.float32)
    for core in range(2):
        for chip in range(8):
            for o in range(SHARE):
                order[core, chip * SHARE + o, (chip * 2 + core) * SHARE + o] = 1.0
    return order


def per_device(
    features,
    stale_edges,
    conv_weight,
    conv_bias,
    first_gain,
    first_shift,
    query_weight,
    key_weight,
    value_weight,
    out_weight,
    out_bias,
    second_gain,
    second_shift,
    geglu_weight,
    geglu_bias,
    down_weight,
    down_bias,
):
    frame = ("x", "yh", "c")
    patch = ("yl", "z")
    packed = call(pack_weight_kernel, (SLOT, 3 * TAPS_PAD), 10**6)(
        conv_weight.transpose(0, 1, 3, 2)
    )
    mirrored = [(h * 4 + l, (1 - h) * 4 + 3 - l) for h in range(2) for l in range(4)]
    other = lax.ppermute(packed, ("yh", "yl"), mirrored)
    pair = jnp.stack([packed, other])
    ring = [pair] + [
        lax.ppermute(pair, "x", [((x + j) % 4, x) for x in range(4)]) for j in (1, 2, 3)
    ]
    weight = jnp.concatenate(ring)
    x, yh, c = (lax.axis_index(a) for a in frame)
    chips = jnp.stack([((x + jx) % 4) * 2 + (yh ^ jy) for jx in range(4) for jy in range(2)])
    lane = jnp.arange(SLOT)[None, :]
    target = jnp.where(lane < SHARE, chips[:, None] * SHARE + lane, -1).reshape(-1, 1)
    chosen = target == jnp.arange(CH // 2)[None, :]
    sel = chosen.astype(jnp.bfloat16)
    core_bias = jnp.where(c == 0, *(conv_bias.reshape(8, 2, SHARE)[:, i].reshape(1, -1) for i in range(2)))
    slot_bias = jnp.sum(jnp.where(chosen, core_bias, 0.0), axis=1)[None, :]

    above = lax.ppermute(
        stale_edges[:, 1].transpose(0, 2, 1), patch, [(i, i + 1) for i in range(PATCHES - 1)]
    )
    below = lax.ppermute(
        stale_edges[:, 0].transpose(0, 2, 1), patch, [(i + 1, i) for i in range(PATCHES - 1)]
    )
    tokens = call(tokens_kernel, (4 * COLS, TAPS_PAD), 10**6)(
        above, features[:, 0].transpose(0, 2, 1), below
    )
    sibling = lax.ppermute(tokens, "c", [(0, 1), (1, 0)])
    outgoing = call(conv_kernel, (16, 16, 2 * CH), 10**9)(tokens, sibling, weight, slot_bias, sel)
    owned = lax.all_to_all(outgoing, frame, 0, 0, tiled=True)
    done = call(
        block_kernel,
        (8, 2, 16, 2 * CH),
        2 * 10**9,
        [pltpu.VMEM((2, 5, 128, 128), jnp.float32), pltpu.VMEM((512, CH), jnp.bfloat16)],
    )(
        owned,
        jnp.asarray(channel_order(), jnp.bfloat16),
        jnp.asarray(position_rows()),
        first_gain[None],
        first_shift[None],
        query_weight,
        key_weight,
        value_weight,
        out_weight,
        out_bias[None],
        second_gain[None],
        second_shift[None],
        geglu_weight,
        geglu_bias[None],
        down_weight,
        down_bias[None],
    )
    returned = lax.all_to_all(done.reshape(16, 16, 2 * CH), frame, 0, 0, tiled=True)
    result = call(finish_kernel, (4, CH, COLS), 10**6)(returned)
    return result.transpose(0, 2, 1)[:, None]


def solution(mesh):
    split = Mesh(mesh.devices.reshape(4, 2, 2, 4, 8), ("x", "yh", "c", "yl", "z"))
    frame, patch = ("x", "yh", "c"), ("yl", "z")
    return jax.shard_map(
        per_device,
        mesh=split,
        in_specs=(P(frame, patch), P(frame, patch), P(None, None, None, frame)) + (P(),) * 14,
        out_specs=P(frame, patch),
        check_vma=False,
    )
```

```python
import functools
import math

import jax
import jax.numpy as jnp
import numpy as np
from jax import lax
from jax.experimental import pallas as pl
from jax.experimental.pallas import tpu as pltpu
from jax.sharding import Mesh, PartitionSpec as P

HEADS = 8
CH = 320
FF = 1280
TAPS_IN = 960
TAPS_PAD = 1024
SHARE = 20
PIECE = 768
FRAMES = 64
COLS = 128
PATCHES = 32
TOKENS_FLOPS = 2*10**10
MIB = 1024 * 1024


def pack_weight_kernel(w_ref, out_ref):
    blank = jnp.zeros((SHARE, TAPS_PAD - TAPS_IN), jnp.float32)
    rows = jnp.concatenate(
        [
            part
            for b in range(3)
            for part in [w_ref[a, b].astype(jnp.float32) for a in range(3)] + [blank]
        ],
        axis=1,
    )
    last = jnp.concatenate([rows[16:, q * PIECE : (q + 1) * PIECE] for q in range(4)], axis=0)
    out_ref[...] = jnp.concatenate([rows[:16], last], axis=1).astype(jnp.bfloat16)


def fan_kernel(own_ref, other_ref, place_ref, out_ref):
    y = place_ref[1]
    for x in range(4):
        out_ref[x, y] = own_ref[...]
        out_ref[x, 1 - y] = other_ref[...]


def tokens_kernel(above_ref, band_ref, below_ref, out_ref):
    blank = jnp.zeros((TAPS_PAD - TAPS_IN, COLS), jnp.bfloat16)
    for f in range(4):
        stacked = jnp.concatenate([above_ref[f], band_ref[f], below_ref[f], blank], axis=0)
        out_ref[f * COLS : (f + 1) * COLS, :] = stacked.T


def convolve(x_ref, w_ref, bias):
    x = x_ref[...]
    tokens = x.shape[0]
    position = lax.broadcasted_iota(jnp.int32, (tokens, 1), 0) % COLS
    split = w_ref[:, :, 3 * TAPS_PAD :].astype(jnp.float32)
    last = jnp.concatenate(
        [
            jnp.concatenate([split[chip, q * 4 : (q + 1) * 4] for chip in range(8)], axis=0)
            for q in range(4)
        ],
        axis=1,
    ).astype(jnp.bfloat16)

    def taps(b):
        cols = slice(b * TAPS_PAD, (b + 1) * TAPS_PAD)
        weight = jnp.concatenate([w_ref[:, :, cols].reshape(-1, TAPS_PAD), last[:, cols]], axis=0)
        return lax.dot_general(
            x, weight, (((1,), (1,)), ((), ())), preferred_element_type=jnp.float32
        )

    left = jnp.where(position == 0, 0.0, pltpu.roll(taps(0), 1, 0))
    right = jnp.where(position == COLS - 1, 0.0, pltpu.roll(taps(2), tokens - 1, 0))
    return taps(1) + left + right + bias


def conv_first_kernel(x_ref, w_ref, bias_ref, order_ref, out_ref):
    rows = convolve(x_ref, w_ref, bias_ref[:1, : CH // 2]).astype(jnp.bfloat16)
    out_ref[...] = jnp.dot(rows, order_ref[: CH // 2, :], preferred_element_type=jnp.float32)


def conv_second_kernel(x_ref, w_ref, bias_ref, order_ref, first_ref, out_ref):
    rows = convolve(x_ref, w_ref, bias_ref[1:2, : CH // 2]).astype(jnp.bfloat16)
    ordered = first_ref[...] + jnp.dot(
        rows, order_ref[CH // 2 :, :], preferred_element_type=jnp.float32
    )
    by_owner = ordered.reshape(2, 2, 16, 8, CH)
    both = jnp.concatenate([by_owner[0], by_owner[1]], axis=-1)
    for k in range(16):
        out_ref[k] = jnp.concatenate([both[0, k], both[1, k]], axis=0).astype(jnp.bfloat16)


def norm_rows(values, gain, shift):
    average = jnp.mean(values, axis=-1, keepdims=True)
    centred = values - average
    variance = jnp.mean(centred * centred, axis=-1, keepdims=True)
    return centred * lax.rsqrt(variance + 1e-05) * gain + shift


def conv_params_kernel(bias_ref, place_ref, sides_ref, order_ref):
    core = place_ref[2]
    bias = bias_ref[...]
    by_core = []
    for i in range(2):
        shares = [bias[:, (chip * 2 + i) * SHARE :][:, :SHARE] for chip in range(8)]
        by_core.append(
            jnp.concatenate([s[:, :16] for s in shares] + [s[:, 16:] for s in shares], axis=1)
        )
    sides_ref[:1, : CH // 2] = jnp.where(core == 0, by_core[0], by_core[1])
    sides_ref[1:2, : CH // 2] = jnp.where(core == 0, by_core[1], by_core[0])
    row = lax.broadcasted_iota(jnp.int32, (CH, CH), 0)
    owner = jnp.where(row < CH // 2, core, 1 - core)
    row = jnp.where(row < CH // 2, row, row - CH // 2)
    chip = jnp.where(row < 128, row >> 4, (row - 128) >> 2)
    share = jnp.where(row < 128, row & 15, 16 + (row & 3))
    channel = (chip * 2 + owner) * SHARE + share
    here = channel == lax.broadcasted_iota(jnp.int32, (CH, CH), 1)
    order_ref[...] = jnp.where(here, 1.0, 0.0).astype(jnp.bfloat16)


def block_params_kernel(*refs):
    query, key, value, out = refs[:4]
    rows = refs[4:11]
    spread_ref, square_ref, vectors_ref = refs[11:]
    source = lax.broadcasted_iota(jnp.int32, (CH, 512), 0)
    lane = lax.broadcasted_iota(jnp.int32, (CH, 512), 1)
    there = ((lane & 63) < 40) & (source == (lane >> 6) * 40 + (lane & 63))
    spread = jnp.where(there, 1.0, 0.0).astype(jnp.bfloat16)
    for i, part in enumerate((query, key)):
        spread_ref[:, i * 512 : (i + 1) * 512] = jnp.dot(
            part[...], spread, preferred_element_type=jnp.float32
        ).astype(jnp.bfloat16)
    square_ref[:CH, :] = value[...].astype(jnp.float32).T.astype(jnp.bfloat16)
    square_ref[CH:, :] = out[...]
    vectors_ref[:FRAMES, :] = rows[0][...]
    for i, row in enumerate(rows[1:]):
        vectors_ref[FRAMES + i : FRAMES + i + 1, :] = row[...]
    vectors_ref[FRAMES + 6 :, :] = jnp.zeros((2, CH), jnp.float32)


def attention_kernel(x_ref, spread_ref, square_ref, vectors_ref, middle_ref, rows_ref, context_ref):
    first_gain, first_shift, out_bias = (
        vectors_ref[FRAMES + i : FRAMES + i + 1, :] for i in range(3)
    )
    pixels = 8
    blocks = 2 * CH // 128
    received = x_ref[...].astype(jnp.float32).reshape(256, 2 * CH)
    for i in range(blocks):
        rows_ref[i] = received[:, i * 128 : (i + 1) * 128]
    pieces = []
    for p in range(pixels):
        both = jnp.concatenate(
            [rows_ref[i, pl.ds(p, 32, stride=pixels), :] for i in range(blocks)], axis=1
        )
        pieces += [both[:, :CH], both[:, CH:]]
    x = jnp.concatenate(pieces, axis=0)
    position = vectors_ref[:FRAMES, :]
    normed = norm_rows(x, first_gain, first_shift).reshape(pixels, FRAMES, CH)
    normed = (normed + position[None]).reshape(pixels * FRAMES, CH).astype(jnp.bfloat16)

    queries, key_rows = (
        jnp.dot(
            normed, spread_ref[:, i * 512 : (i + 1) * 512], preferred_element_type=jnp.float32
        ).astype(jnp.bfloat16)
        for i in range(2)
    )
    across = (((1,), (1,)), ((), ()))
    values = lax.dot_general(
        square_ref[:CH, :], normed, across, preferred_element_type=jnp.float32
    ).astype(jnp.bfloat16)
    scale = 1.0 / math.sqrt(CH // HEADS)
    head_of = lax.broadcasted_iota(jnp.int32, (1, 256), 1) >> 6
    units = [(p, quad) for p in range(pixels) for quad in range(2)]
    scores = []
    for p, quad in units:
        rows = slice(p * FRAMES, (p + 1) * FRAMES)
        lanes = slice(quad * 256, (quad + 1) * 256)
        query = queries[rows, lanes]
        stacked = jnp.concatenate(
            [jnp.where(head_of == h, query, jnp.zeros_like(query)) for h in range(4)], axis=0
        )
        scores.append(
            lax.dot_general(
                key_rows[rows, lanes], stacked, across, preferred_element_type=jnp.float32
            )
        )
    scores = jnp.concatenate(scores, axis=1)
    expo = jnp.exp((scores - jnp.max(scores, axis=0, keepdims=True)) * scale)
    probs = (expo * (1.0 / jnp.sum(expo, axis=0, keepdims=True))).astype(jnp.bfloat16)
    contexts = []
    for i, (p, quad) in enumerate(units):
        rows = slice(p * FRAMES, (p + 1) * FRAMES)
        mixed = jnp.dot(
            values[quad * 160 : (quad + 1) * 160, rows],
            probs[:, i * 256 : (i + 1) * 256],
            preferred_element_type=jnp.float32,
        )
        for h in range(4):
            contexts.append(mixed[h * 40 : (h + 1) * 40, h * FRAMES : (h + 1) * FRAMES])
    for p in range(0, pixels, 2):
        left = jnp.concatenate(contexts[p * HEADS : (p + 1) * HEADS], axis=0)
        right = jnp.concatenate(contexts[(p + 1) * HEADS : (p + 2) * HEADS], axis=0)
        context_ref[:, p * FRAMES : (p + 2) * FRAMES] = jnp.concatenate(
            [left, right], axis=1
        ).astype(jnp.bfloat16)
    attn_out = (
        lax.dot_general(
            context_ref[...],
            square_ref[CH:, :],
            (((0,), (0,)), ((), ())),
            preferred_element_type=jnp.float32,
        )
        + out_bias
    ).astype(jnp.bfloat16)
    middle_ref[...] = (x + attn_out.astype(jnp.float32)).astype(jnp.bfloat16)


def feed_kernel(middle_ref, vectors_ref, geglu_ref, geglu_bias_ref, down_ref, out_ref, rows_ref):
    pixels = 8
    blocks = 2 * CH // 128
    second_gain, second_shift, down_bias = (
        vectors_ref[FRAMES + i : FRAMES + i + 1, :] for i in range(3, 6)
    )
    middle = middle_ref[...].astype(jnp.float32)
    normed_two = norm_rows(middle, second_gain, second_shift).astype(jnp.bfloat16)
    total = middle + down_bias
    step = 256
    for start in range(0, FF, step):
        lanes = slice(start, start + step)
        gates = slice(FF + start, FF + start + step)
        value = (
            jnp.dot(normed_two, geglu_ref[:, lanes], preferred_element_type=jnp.float32)
            + geglu_bias_ref[:, lanes]
        )
        gate = (
            jnp.dot(normed_two, geglu_ref[:, gates], preferred_element_type=jnp.float32)
            + geglu_bias_ref[:, gates]
        )
        hidden = value * (0.5 * gate * (1.0 + lax.erf(gate * (1.0 / math.sqrt(2.0)))))
        total = total + lax.dot_general(
            hidden.astype(jnp.bfloat16),
            down_ref[:, lanes],
            (((1,), (1,)), ((), ())),
            preferred_element_type=jnp.float32,
        )
    for p in range(pixels):
        near = total[p * FRAMES : p * FRAMES + 32]
        far = total[p * FRAMES + 32 : (p + 1) * FRAMES]
        both = jnp.concatenate([near, far], axis=1)
        for i in range(blocks):
            rows_ref[i, pl.ds(p, 32, stride=pixels), :] = both[:, i * 128 : (i + 1) * 128]
    for i in range(blocks):
        out_ref[:, :, i * 128 : (i + 1) * 128] = (
            rows_ref[i].astype(jnp.bfloat16).reshape(16, 16, 128)
        )


def finish_kernel(x_ref, out_ref):
    received = x_ref[...].astype(jnp.float32)
    for half in range(2):
        lanes = slice(half * CH, (half + 1) * CH)
        for f in range(2):
            rows = received[:, f * 8 : (f + 1) * 8, lanes].reshape(COLS, CH)
            out_ref[half * 2 + f] = rows.T.astype(jnp.bfloat16)


def call(kernel, out_shape, flops, scratch=(), in_specs=None, vmem=8):
    many = isinstance(out_shape, list)
    shapes = [jax.ShapeDtypeStruct(*o) for o in out_shape] if many else out_shape
    spaces = {}
    if in_specs is not None:
        spaces["in_specs"] = [pl.BlockSpec(memory_space=i or pltpu.VMEM) for i in in_specs]
    return pl.pallas_call(
        kernel,
        out_shape=shapes if many else jax.ShapeDtypeStruct(out_shape, jnp.bfloat16),
        scratch_shapes=list(scratch),
        compiler_params=pltpu.CompilerParams(vmem_limit_bytes=vmem * MIB),
        cost_estimate=pl.CostEstimate(flops=flops, bytes_accessed=4 * MIB, transcendentals=0),
        **spaces,
    )


def position_rows():
    frames = np.array([d * 4 + high * 2 + low for high in range(2) for d in range(16) for low in range(2)])
    rates = 10000.0 ** (-2.0 * np.arange(CH // 2) / CH)
    angles = frames[:, None] * rates[None, :]
    return np.stack([np.sin(angles), np.cos(angles)], axis=-1).reshape(FRAMES, CH).astype(np.float32)


def per_device(
    features,
    stale_edges,
    conv_weight,
    conv_bias,
    first_gain,
    first_shift,
    query_weight,
    key_weight,
    value_weight,
    out_weight,
    out_bias,
    second_gain,
    second_shift,
    geglu_weight,
    geglu_bias,
    down_weight,
    down_bias,
):
    frame = ("x", "yh", "c")
    patch = ("yl", "z")
    packed = call(pack_weight_kernel, (16, 3 * TAPS_PAD + PIECE), 10**6)(
        conv_weight.transpose(0, 1, 3, 2)
    )
    mirrored = [(h * 4 + l, (1 - h) * 4 + 3 - l) for h in range(2) for l in range(4)]
    other = lax.ppermute(packed, ("yh", "yl"), mirrored)
    place = jnp.stack([lax.axis_index(a) for a in frame]).astype(jnp.int32)
    fanned = call(
        fan_kernel, (4, 2, 16, 3 * TAPS_PAD + PIECE), 10**6, in_specs=[None, None, pltpu.SMEM]
    )(packed, other, place)
    weight = lax.all_to_all(fanned, "x", 0, 0, tiled=True).reshape(8, 16, 3 * TAPS_PAD + PIECE)

    theirs = lax.ppermute(weight, "c", [(0, 1), (1, 0)])

    rims = stale_edges.transpose(0, 1, 3, 2)
    above = lax.ppermute(rims[:, 1], patch, [(i, i + 1) for i in range(PATCHES - 1)])
    below = lax.ppermute(rims[:, 0], patch, [(i + 1, i) for i in range(PATCHES - 1)])

    sides, order = call(
        conv_params_kernel,
        [((8, CH), jnp.float32), ((CH, CH), jnp.bfloat16)],
        10**6,
        in_specs=[None, pltpu.SMEM],
    )(conv_bias[None], place)
    tokens = call(tokens_kernel, (4 * COLS, TAPS_PAD), TOKENS_FLOPS)(
        above, features[:, 0].transpose(0, 2, 1), below
    )
    first = call(conv_first_kernel, [((512, CH), jnp.float32)], 10**9, vmem=24)(
        tokens, weight, sides, order
    )[0]
    outgoing = call(conv_second_kernel, (16, 16, 2 * CH), 10**9, vmem=24)(
        tokens, theirs, sides, order, first
    )
    owned = lax.all_to_all(outgoing, frame, 0, 0, tiled=True)
    rows = [first_gain, first_shift, out_bias, second_gain, second_shift, down_bias]
    query_weight, outgoing = lax.optimization_barrier((query_weight, outgoing))
    spread, square, vectors = call(
        block_params_kernel,
        [
            ((CH, 1024), jnp.bfloat16),
            ((2 * CH, CH), jnp.bfloat16),
            ((FRAMES + 8, CH), jnp.float32),
        ],
        10**6,
    )(
        query_weight,
        key_weight,
        value_weight,
        out_weight,
        position_rows(),
        *(row[None] for row in rows),
    )
    by_pixel = pltpu.VMEM((5, 256, 128), jnp.float32)
    middle = call(
        attention_kernel,
        (512, CH),
        10**9,
        [by_pixel, pltpu.VMEM((CH, 512), jnp.bfloat16)],
        vmem=24,
    )(owned, spread, square, vectors)
    done = call(feed_kernel, (16, 16, 2 * CH), 10**9, [by_pixel], vmem=24)(
        middle, vectors, geglu_weight, geglu_bias[None], down_weight.T
    )
    returned = lax.all_to_all(done, frame, 0, 0, tiled=True)
    result = call(finish_kernel, (4, CH, COLS), 10**6)(returned)
    return result.transpose(0, 2, 1)[:, None]


def solution(mesh):
    split = Mesh(mesh.devices.reshape(4, 2, 2, 4, 8), ("x", "yh", "c", "yl", "z"))
    frame, patch = ("x", "yh", "c"), ("yl", "z")
    return jax.shard_map(
        per_device,
        mesh=split,
        in_specs=(P(frame, patch), P(frame, patch), P(None, None, None, frame)) + (P(),) * 14,
        out_specs=P(frame, patch),
        check_vma=False,
    )
```

```python
import functools
import math

import jax
import jax.numpy as jnp
import numpy as np
from jax import lax
from jax.experimental import pallas as pl
from jax.experimental.pallas import tpu as pltpu
from jax.sharding import Mesh, PartitionSpec as P

HEADS = 8
CH = 320
FF = 1280
TAPS_IN = 960
TAPS_PAD = 1024
SHARE = 20
PIECE = 768
FRAMES = 64
COLS = 128
PATCHES = 32
TOKENS_FLOPS = 5*10**9
FAN_FLOPS = 10**6
MIB = 1024 * 1024


def pack_weight_kernel(w_ref, out_ref):
    blank = jnp.zeros((SHARE, TAPS_PAD - TAPS_IN), jnp.float32)
    rows = jnp.concatenate(
        [
            part
            for b in range(3)
            for part in [w_ref[a, b].astype(jnp.float32) for a in range(3)] + [blank]
        ],
        axis=1,
    )
    last = jnp.concatenate([rows[16:, q * PIECE : (q + 1) * PIECE] for q in range(4)], axis=0)
    out_ref[...] = jnp.concatenate([rows[:16], last], axis=1).astype(jnp.bfloat16)


def fan_kernel(own_ref, other_ref, place_ref, out_ref):
    y = place_ref[1]
    for x in range(4):
        out_ref[x, y] = own_ref[...]
        out_ref[x, 1 - y] = other_ref[...]


def tokens_kernel(*refs):
    *parts, out_ref = refs
    for f in range(4):
        stacked = [part[f] for part in parts]
        blank = out_ref.shape[1] - CH * len(parts)
        if blank:
            stacked.append(jnp.zeros((blank, COLS), jnp.bfloat16))
        out_ref[f * COLS : (f + 1) * COLS, :] = jnp.concatenate(stacked, axis=0).T


def convolve(upper_ref, below_ref, w_ref, bias):
    x = jnp.concatenate([upper_ref[...], below_ref[...]], axis=1)
    tokens = x.shape[0]
    position = lax.broadcasted_iota(jnp.int32, (tokens, 1), 0) % COLS
    split = w_ref[:, :, 3 * TAPS_PAD :].astype(jnp.float32)
    last = jnp.concatenate(
        [
            jnp.concatenate([split[chip, q * 4 : (q + 1) * 4] for chip in range(8)], axis=0)
            for q in range(4)
        ],
        axis=1,
    ).astype(jnp.bfloat16)

    def taps(b):
        cols = slice(b * TAPS_PAD, (b + 1) * TAPS_PAD)
        weight = jnp.concatenate([w_ref[:, :, cols].reshape(-1, TAPS_PAD), last[:, cols]], axis=0)
        return lax.dot_general(
            x, weight, (((1,), (1,)), ((), ())), preferred_element_type=jnp.float32
        )

    left = jnp.where(position == 0, 0.0, pltpu.roll(taps(0), 1, 0))
    right = jnp.where(position == COLS - 1, 0.0, pltpu.roll(taps(2), tokens - 1, 0))
    return taps(1) + left + right + bias


def conv_first_kernel(upper_ref, below_ref, w_ref, bias_ref, order_ref, out_ref):
    rows = convolve(upper_ref, below_ref, w_ref, bias_ref[:1, : CH // 2]).astype(jnp.bfloat16)
    out_ref[...] = jnp.dot(rows, order_ref[: CH // 2, :], preferred_element_type=jnp.float32)


def conv_second_kernel(upper_ref, below_ref, w_ref, bias_ref, order_ref, first_ref, out_ref):
    rows = convolve(upper_ref, below_ref, w_ref, bias_ref[1:2, : CH // 2]).astype(jnp.bfloat16)
    ordered = first_ref[...] + jnp.dot(
        rows, order_ref[CH // 2 :, :], preferred_element_type=jnp.float32
    )
    by_owner = ordered.reshape(2, 2, 16, 8, CH)
    both = jnp.concatenate([by_owner[0], by_owner[1]], axis=-1)
    for k in range(16):
        out_ref[k] = jnp.concatenate([both[0, k], both[1, k]], axis=0).astype(jnp.bfloat16)


def norm_rows(values, gain, shift):
    average = jnp.mean(values, axis=-1, keepdims=True)
    centred = values - average
    variance = jnp.mean(centred * centred, axis=-1, keepdims=True)
    return centred * lax.rsqrt(variance + 1e-05) * gain + shift


def conv_params_kernel(bias_ref, place_ref, sides_ref, order_ref):
    core = place_ref[2]
    bias = bias_ref[...]
    by_core = []
    for i in range(2):
        shares = [bias[:, (chip * 2 + i) * SHARE :][:, :SHARE] for chip in range(8)]
        by_core.append(
            jnp.concatenate([s[:, :16] for s in shares] + [s[:, 16:] for s in shares], axis=1)
        )
    sides_ref[:1, : CH // 2] = jnp.where(core == 0, by_core[0], by_core[1])
    sides_ref[1:2, : CH // 2] = jnp.where(core == 0, by_core[1], by_core[0])
    row = lax.broadcasted_iota(jnp.int32, (CH, CH), 0)
    owner = jnp.where(row < CH // 2, core, 1 - core)
    row = jnp.where(row < CH // 2, row, row - CH // 2)
    chip = jnp.where(row < 128, row >> 4, (row - 128) >> 2)
    share = jnp.where(row < 128, row & 15, 16 + (row & 3))
    channel = (chip * 2 + owner) * SHARE + share
    here = channel == lax.broadcasted_iota(jnp.int32, (CH, CH), 1)
    order_ref[...] = jnp.where(here, 1.0, 0.0).astype(jnp.bfloat16)


def block_params_kernel(*refs):
    query, key, value, out = refs[:4]
    rows = refs[4:11]
    spread_ref, square_ref, vectors_ref = refs[11:]
    source = lax.broadcasted_iota(jnp.int32, (CH, 512), 0)
    lane = lax.broadcasted_iota(jnp.int32, (CH, 512), 1)
    there = ((lane & 63) < 40) & (source == (lane >> 6) * 40 + (lane & 63))
    spread = jnp.where(there, 1.0, 0.0).astype(jnp.bfloat16)
    for i, part in enumerate((query, key)):
        spread_ref[:, i * 512 : (i + 1) * 512] = jnp.dot(
            part[...], spread, preferred_element_type=jnp.float32
        ).astype(jnp.bfloat16)
    square_ref[:CH, :] = value[...].astype(jnp.float32).T.astype(jnp.bfloat16)
    square_ref[CH:, :] = out[...]
    vectors_ref[:FRAMES, :] = rows[0][...]
    for i, row in enumerate(rows[1:]):
        vectors_ref[FRAMES + i : FRAMES + i + 1, :] = row[...]
    vectors_ref[FRAMES + 6 :, :] = jnp.zeros((2, CH), jnp.float32)


def attention_kernel(x_ref, spread_ref, square_ref, vectors_ref, middle_ref, rows_ref, context_ref):
    first_gain, first_shift, out_bias = (
        vectors_ref[FRAMES + i : FRAMES + i + 1, :] for i in range(3)
    )
    pixels = 8
    blocks = 2 * CH // 128
    received = x_ref[...].astype(jnp.float32).reshape(256, 2 * CH)
    for i in range(blocks):
        rows_ref[i] = received[:, i * 128 : (i + 1) * 128]
    pieces = []
    for p in range(pixels):
        both = jnp.concatenate(
            [rows_ref[i, pl.ds(p, 32, stride=pixels), :] for i in range(blocks)], axis=1
        )
        pieces += [both[:, :CH], both[:, CH:]]
    x = jnp.concatenate(pieces, axis=0)
    position = vectors_ref[:FRAMES, :]
    normed = norm_rows(x, first_gain, first_shift).reshape(pixels, FRAMES, CH)
    normed = (normed + position[None]).reshape(pixels * FRAMES, CH).astype(jnp.bfloat16)

    queries, key_rows = (
        jnp.dot(
            normed, spread_ref[:, i * 512 : (i + 1) * 512], preferred_element_type=jnp.float32
        ).astype(jnp.bfloat16)
        for i in range(2)
    )
    across = (((1,), (1,)), ((), ()))
    values = lax.dot_general(
        square_ref[:CH, :], normed, across, preferred_element_type=jnp.float32
    ).astype(jnp.bfloat16)
    scale = 1.0 / math.sqrt(CH // HEADS)
    head_of = lax.broadcasted_iota(jnp.int32, (1, 256), 1) >> 6
    units = [(p, quad) for p in range(pixels) for quad in range(2)]
    scores = []
    for p, quad in units:
        rows = slice(p * FRAMES, (p + 1) * FRAMES)
        lanes = slice(quad * 256, (quad + 1) * 256)
        query = queries[rows, lanes]
        stacked = jnp.concatenate(
            [jnp.where(head_of == h, query, jnp.zeros_like(query)) for h in range(4)], axis=0
        )
        scores.append(
            lax.dot_general(
                key_rows[rows, lanes], stacked, across, preferred_element_type=jnp.float32
            )
        )
    scores = jnp.concatenate(scores, axis=1)
    expo = jnp.exp((scores - jnp.max(scores, axis=0, keepdims=True)) * scale)
    probs = (expo * (1.0 / jnp.sum(expo, axis=0, keepdims=True))).astype(jnp.bfloat16)
    contexts = []
    for i, (p, quad) in enumerate(units):
        rows = slice(p * FRAMES, (p + 1) * FRAMES)
        mixed = jnp.dot(
            values[quad * 160 : (quad + 1) * 160, rows],
            probs[:, i * 256 : (i + 1) * 256],
            preferred_element_type=jnp.float32,
        )
        for h in range(4):
            contexts.append(mixed[h * 40 : (h + 1) * 40, h * FRAMES : (h + 1) * FRAMES])
    for p in range(0, pixels, 2):
        left = jnp.concatenate(contexts[p * HEADS : (p + 1) * HEADS], axis=0)
        right = jnp.concatenate(contexts[(p + 1) * HEADS : (p + 2) * HEADS], axis=0)
        context_ref[:, p * FRAMES : (p + 2) * FRAMES] = jnp.concatenate(
            [left, right], axis=1
        ).astype(jnp.bfloat16)
    attn_out = (
        lax.dot_general(
            context_ref[...],
            square_ref[CH:, :],
            (((0,), (0,)), ((), ())),
            preferred_element_type=jnp.float32,
        )
        + out_bias
    ).astype(jnp.bfloat16)
    middle_ref[...] = (x + attn_out.astype(jnp.float32)).astype(jnp.bfloat16)


def feed_kernel(middle_ref, vectors_ref, geglu_ref, geglu_bias_ref, down_ref, out_ref, rows_ref):
    pixels = 8
    blocks = 2 * CH // 128
    second_gain, second_shift, down_bias = (
        vectors_ref[FRAMES + i : FRAMES + i + 1, :] for i in range(3, 6)
    )
    middle = middle_ref[...].astype(jnp.float32)
    normed_two = norm_rows(middle, second_gain, second_shift).astype(jnp.bfloat16)
    total = middle + down_bias
    step = 256
    for start in range(0, FF, step):
        lanes = slice(start, start + step)
        gates = slice(FF + start, FF + start + step)
        value = (
            jnp.dot(normed_two, geglu_ref[:, lanes], preferred_element_type=jnp.float32)
            + geglu_bias_ref[:, lanes]
        )
        gate = (
            jnp.dot(normed_two, geglu_ref[:, gates], preferred_element_type=jnp.float32)
            + geglu_bias_ref[:, gates]
        )
        hidden = value * (0.5 * gate * (1.0 + lax.erf(gate * (1.0 / math.sqrt(2.0)))))
        total = total + lax.dot_general(
            hidden.astype(jnp.bfloat16),
            down_ref[:, lanes],
            (((1,), (1,)), ((), ())),
            preferred_element_type=jnp.float32,
        )
    for p in range(pixels):
        near = total[p * FRAMES : p * FRAMES + 32]
        far = total[p * FRAMES + 32 : (p + 1) * FRAMES]
        both = jnp.concatenate([near, far], axis=1)
        for i in range(blocks):
            rows_ref[i, pl.ds(p, 32, stride=pixels), :] = both[:, i * 128 : (i + 1) * 128]
    for i in range(blocks):
        out_ref[:, :, i * 128 : (i + 1) * 128] = (
            rows_ref[i].astype(jnp.bfloat16).reshape(16, 16, 128)
        )


def finish_kernel(x_ref, out_ref):
    received = x_ref[...].astype(jnp.float32)
    for half in range(2):
        lanes = slice(half * CH, (half + 1) * CH)
        for f in range(2):
            rows = received[:, f * 8 : (f + 1) * 8, lanes].reshape(COLS, CH)
            out_ref[half * 2 + f] = rows.T.astype(jnp.bfloat16)


def call(kernel, out_shape, flops, scratch=(), in_specs=None, vmem=8):
    many = isinstance(out_shape, list)
    shapes = [jax.ShapeDtypeStruct(*o) for o in out_shape] if many else out_shape
    spaces = {}
    if in_specs is not None:
        spaces["in_specs"] = [pl.BlockSpec(memory_space=i or pltpu.VMEM) for i in in_specs]
    return pl.pallas_call(
        kernel,
        out_shape=shapes if many else jax.ShapeDtypeStruct(out_shape, jnp.bfloat16),
        scratch_shapes=list(scratch),
        compiler_params=pltpu.CompilerParams(vmem_limit_bytes=vmem * MIB),
        cost_estimate=pl.CostEstimate(flops=flops, bytes_accessed=4 * MIB, transcendentals=0),
        **spaces,
    )


def position_rows():
    frames = np.array([d * 4 + high * 2 + low for high in range(2) for d in range(16) for low in range(2)])
    rates = 10000.0 ** (-2.0 * np.arange(CH // 2) / CH)
    angles = frames[:, None] * rates[None, :]
    return np.stack([np.sin(angles), np.cos(angles)], axis=-1).reshape(FRAMES, CH).astype(np.float32)


def per_device(
    features,
    stale_edges,
    conv_weight,
    conv_bias,
    first_gain,
    first_shift,
    query_weight,
    key_weight,
    value_weight,
    out_weight,
    out_bias,
    second_gain,
    second_shift,
    geglu_weight,
    geglu_bias,
    down_weight,
    down_bias,
):
    frame = ("x", "yh", "c")
    patch = ("yl", "z")
    packed = call(pack_weight_kernel, (16, 3 * TAPS_PAD + PIECE), 10**6)(
        conv_weight.transpose(0, 1, 3, 2)
    )
    mirrored = [(h * 4 + l, (1 - h) * 4 + 3 - l) for h in range(2) for l in range(4)]
    other = lax.ppermute(packed, ("yh", "yl"), mirrored)
    place = jnp.stack([lax.axis_index(a) for a in frame]).astype(jnp.int32)
    fanned = call(
        fan_kernel, (4, 2, 16, 3 * TAPS_PAD + PIECE), FAN_FLOPS, in_specs=[None, None, pltpu.SMEM]
    )(packed, other, place)
    weight = lax.all_to_all(fanned, "x", 0, 0, tiled=True).reshape(8, 16, 3 * TAPS_PAD + PIECE)

    rims = stale_edges.transpose(0, 1, 3, 2)
    above = lax.ppermute(rims[:, 1], patch, [(i, i + 1) for i in range(PATCHES - 1)])
    below = lax.ppermute(rims[:, 0], patch, [(i + 1, i) for i in range(PATCHES - 1)])

    sides, order = call(
        conv_params_kernel,
        [((8, CH), jnp.float32), ((CH, CH), jnp.bfloat16)],
        10**6,
        in_specs=[None, pltpu.SMEM],
    )(conv_bias[None], place)
    band = features[:, 0].transpose(0, 2, 1)
    upper = call(tokens_kernel, (4 * COLS, 2 * CH), TOKENS_FLOPS)(above, band)
    under = call(tokens_kernel, (4 * COLS, TAPS_PAD - 2 * CH), 12*10**9)(below)
    weight, upper = lax.optimization_barrier((weight, upper))
    theirs = lax.ppermute(weight, "c", [(0, 1), (1, 0)])
    first = call(conv_first_kernel, [((512, CH), jnp.float32)], 10**9, vmem=24)(
        upper, under, weight, sides, order
    )[0]
    outgoing = call(conv_second_kernel, (16, 16, 2 * CH), 10**9, vmem=24)(
        upper, under, theirs, sides, order, first
    )
    owned = lax.all_to_all(outgoing, frame, 0, 0, tiled=True)
    rows = [first_gain, first_shift, out_bias, second_gain, second_shift, down_bias]
    query_weight, outgoing = lax.optimization_barrier((query_weight, outgoing))
    spread, square, vectors = call(
        block_params_kernel,
        [
            ((CH, 1024), jnp.bfloat16),
            ((2 * CH, CH), jnp.bfloat16),
            ((FRAMES + 8, CH), jnp.float32),
        ],
        10**6,
    )(
        query_weight,
        key_weight,
        value_weight,
        out_weight,
        position_rows(),
        *(row[None] for row in rows),
    )
    by_pixel = pltpu.VMEM((5, 256, 128), jnp.float32)
    middle = call(
        attention_kernel,
        (512, CH),
        10**9,
        [by_pixel, pltpu.VMEM((CH, 512), jnp.bfloat16)],
        vmem=24,
    )(owned, spread, square, vectors)
    done = call(feed_kernel, (16, 16, 2 * CH), 10**9, [by_pixel], vmem=24)(
        middle, vectors, geglu_weight, geglu_bias[None], down_weight.T
    )
    returned = lax.all_to_all(done, frame, 0, 0, tiled=True)
    result = call(finish_kernel, (4, CH, COLS), 10**6)(returned)
    return result.transpose(0, 2, 1)[:, None]


def solution(mesh):
    split = Mesh(mesh.devices.reshape(4, 2, 2, 4, 8), ("x", "yh", "c", "yl", "z"))
    frame, patch = ("x", "yh", "c"), ("yl", "z")
    return jax.shard_map(
        per_device,
        mesh=split,
        in_specs=(P(frame, patch), P(frame, patch), P(None, None, None, frame)) + (P(),) * 14,
        out_specs=P(frame, patch),
        check_vma=False,
    )
```

```python
import functools
import math

import jax
import jax.numpy as jnp
import numpy as np
from jax import lax
from jax.experimental import pallas as pl
from jax.experimental.pallas import tpu as pltpu
from jax.sharding import Mesh, PartitionSpec as P

HEADS = 8
CH = 320
FF = 1280
TAPS_IN = 960
TAPS_PAD = 1024
SHARE = 20
PIECE = 768
FRAMES = 64
COLS = 128
PATCHES = 32
TOKENS_FLOPS = 5*10**9
MIB = 1024 * 1024


def pack_weight_kernel(w_ref, out_ref):
    blank = jnp.zeros((SHARE, TAPS_PAD - TAPS_IN), jnp.float32)
    rows = jnp.concatenate(
        [
            part
            for b in range(3)
            for part in [w_ref[a, b].astype(jnp.float32) for a in range(3)] + [blank]
        ],
        axis=1,
    )
    last = jnp.concatenate([rows[16:, q * PIECE : (q + 1) * PIECE] for q in range(4)], axis=0)
    out_ref[...] = jnp.concatenate([rows[:16], last], axis=1).astype(jnp.bfloat16)


def tokens_kernel(*refs):
    *parts, out_ref = refs
    for f in range(4):
        stacked = [part[f] for part in parts]
        blank = out_ref.shape[1] - CH * len(parts)
        if blank:
            stacked.append(jnp.zeros((blank, COLS), jnp.bfloat16))
        out_ref[f * COLS : (f + 1) * COLS, :] = jnp.concatenate(stacked, axis=0).T


def convolve(upper_ref, below_ref, w_ref, bias):
    x = jnp.concatenate([upper_ref[...], below_ref[...]], axis=1)
    tokens = x.shape[0]
    position = lax.broadcasted_iota(jnp.int32, (tokens, 1), 0) % COLS
    split = w_ref[:, :, 3 * TAPS_PAD :].astype(jnp.float32)
    last = jnp.concatenate(
        [
            jnp.concatenate([split[chip, q * 4 : (q + 1) * 4] for chip in range(8)], axis=0)
            for q in range(4)
        ],
        axis=1,
    ).astype(jnp.bfloat16)

    def taps(b):
        cols = slice(b * TAPS_PAD, (b + 1) * TAPS_PAD)
        weight = jnp.concatenate([w_ref[:, :, cols].reshape(-1, TAPS_PAD), last[:, cols]], axis=0)
        return lax.dot_general(
            x, weight, (((1,), (1,)), ((), ())), preferred_element_type=jnp.float32
        )

    left = jnp.where(position == 0, 0.0, pltpu.roll(taps(0), 1, 0))
    right = jnp.where(position == COLS - 1, 0.0, pltpu.roll(taps(2), tokens - 1, 0))
    return taps(1) + left + right + bias


def conv_first_kernel(upper_ref, below_ref, w_ref, bias_ref, order_ref, out_ref):
    rows = convolve(upper_ref, below_ref, w_ref, bias_ref[:1, : CH // 2]).astype(jnp.bfloat16)
    out_ref[...] = jnp.dot(rows, order_ref[: CH // 2, :], preferred_element_type=jnp.float32)


def conv_second_kernel(upper_ref, below_ref, w_ref, bias_ref, order_ref, first_ref, out_ref):
    rows = convolve(upper_ref, below_ref, w_ref, bias_ref[1:2, : CH // 2]).astype(jnp.bfloat16)
    ordered = first_ref[...] + jnp.dot(
        rows, order_ref[CH // 2 :, :], preferred_element_type=jnp.float32
    )
    by_owner = ordered.reshape(2, 2, 16, 8, CH)
    both = jnp.concatenate([by_owner[0], by_owner[1]], axis=-1)
    for k in range(16):
        out_ref[k] = jnp.concatenate([both[0, k], both[1, k]], axis=0).astype(jnp.bfloat16)


def norm_rows(values, gain, shift):
    average = jnp.mean(values, axis=-1, keepdims=True)
    centred = values - average
    variance = jnp.mean(centred * centred, axis=-1, keepdims=True)
    return centred * lax.rsqrt(variance + 1e-05) * gain + shift


def conv_params_kernel(bias_ref, place_ref, sides_ref, order_ref):
    core = place_ref[2]
    bias = bias_ref[...]
    by_core = []
    for i in range(2):
        shares = [bias[:, (chip * 2 + i) * SHARE :][:, :SHARE] for chip in range(8)]
        by_core.append(
            jnp.concatenate([s[:, :16] for s in shares] + [s[:, 16:] for s in shares], axis=1)
        )
    sides_ref[:1, : CH // 2] = jnp.where(core == 0, by_core[0], by_core[1])
    sides_ref[1:2, : CH // 2] = jnp.where(core == 0, by_core[1], by_core[0])
    row = lax.broadcasted_iota(jnp.int32, (CH, CH), 0)
    owner = jnp.where(row < CH // 2, core, 1 - core)
    row = jnp.where(row < CH // 2, row, row - CH // 2)
    chip = jnp.where(row < 128, row >> 4, (row - 128) >> 2)
    share = jnp.where(row < 128, row & 15, 16 + (row & 3))
    channel = (chip * 2 + owner) * SHARE + share
    here = channel == lax.broadcasted_iota(jnp.int32, (CH, CH), 1)
    order_ref[...] = jnp.where(here, 1.0, 0.0).astype(jnp.bfloat16)


def block_params_kernel(*refs):
    query, key, value, out = refs[:4]
    rows = refs[4:11]
    spread_ref, square_ref, vectors_ref = refs[11:]
    source = lax.broadcasted_iota(jnp.int32, (CH, 512), 0)
    lane = lax.broadcasted_iota(jnp.int32, (CH, 512), 1)
    there = ((lane & 63) < 40) & (source == (lane >> 6) * 40 + (lane & 63))
    spread = jnp.where(there, 1.0, 0.0).astype(jnp.bfloat16)
    for i, part in enumerate((query, key)):
        spread_ref[:, i * 512 : (i + 1) * 512] = jnp.dot(
            part[...], spread, preferred_element_type=jnp.float32
        ).astype(jnp.bfloat16)
    square_ref[:CH, :] = value[...].astype(jnp.float32).T.astype(jnp.bfloat16)
    square_ref[CH:, :] = out[...]
    vectors_ref[:FRAMES, :] = rows[0][...]
    for i, row in enumerate(rows[1:]):
        vectors_ref[FRAMES + i : FRAMES + i + 1, :] = row[...]
    vectors_ref[FRAMES + 6 :, :] = jnp.zeros((2, CH), jnp.float32)


def attention_kernel(x_ref, spread_ref, square_ref, vectors_ref, middle_ref, rows_ref, context_ref):
    first_gain, first_shift, out_bias = (
        vectors_ref[FRAMES + i : FRAMES + i + 1, :] for i in range(3)
    )
    pixels = 8
    blocks = 2 * CH // 128
    received = x_ref[...].astype(jnp.float32).reshape(256, 2 * CH)
    for i in range(blocks):
        rows_ref[i] = received[:, i * 128 : (i + 1) * 128]
    pieces = []
    for p in range(pixels):
        both = jnp.concatenate(
            [rows_ref[i, pl.ds(p, 32, stride=pixels), :] for i in range(blocks)], axis=1
        )
        pieces += [both[:, :CH], both[:, CH:]]
    x = jnp.concatenate(pieces, axis=0)
    position = vectors_ref[:FRAMES, :]
    normed = norm_rows(x, first_gain, first_shift).reshape(pixels, FRAMES, CH)
    normed = (normed + position[None]).reshape(pixels * FRAMES, CH).astype(jnp.bfloat16)

    queries, key_rows = (
        jnp.dot(
            normed, spread_ref[:, i * 512 : (i + 1) * 512], preferred_element_type=jnp.float32
        ).astype(jnp.bfloat16)
        for i in range(2)
    )
    across = (((1,), (1,)), ((), ()))
    values = lax.dot_general(
        square_ref[:CH, :], normed, across, preferred_element_type=jnp.float32
    ).astype(jnp.bfloat16)
    scale = 1.0 / math.sqrt(CH // HEADS)
    head_of = lax.broadcasted_iota(jnp.int32, (1, 256), 1) >> 6
    units = [(p, quad) for p in range(pixels) for quad in range(2)]
    scores = []
    for p, quad in units:
        rows = slice(p * FRAMES, (p + 1) * FRAMES)
        lanes = slice(quad * 256, (quad + 1) * 256)
        query = queries[rows, lanes]
        stacked = jnp.concatenate(
            [jnp.where(head_of == h, query, jnp.zeros_like(query)) for h in range(4)], axis=0
        )
        scores.append(
            lax.dot_general(
                key_rows[rows, lanes], stacked, across, preferred_element_type=jnp.float32
            )
        )
    scores = jnp.concatenate(scores, axis=1)
    expo = jnp.exp((scores - jnp.max(scores, axis=0, keepdims=True)) * scale)
    probs = (expo * (1.0 / jnp.sum(expo, axis=0, keepdims=True))).astype(jnp.bfloat16)
    contexts = []
    for i, (p, quad) in enumerate(units):
        rows = slice(p * FRAMES, (p + 1) * FRAMES)
        mixed = jnp.dot(
            values[quad * 160 : (quad + 1) * 160, rows],
            probs[:, i * 256 : (i + 1) * 256],
            preferred_element_type=jnp.float32,
        )
        for h in range(4):
            contexts.append(mixed[h * 40 : (h + 1) * 40, h * FRAMES : (h + 1) * FRAMES])
    for p in range(0, pixels, 2):
        left = jnp.concatenate(contexts[p * HEADS : (p + 1) * HEADS], axis=0)
        right = jnp.concatenate(contexts[(p + 1) * HEADS : (p + 2) * HEADS], axis=0)
        context_ref[:, p * FRAMES : (p + 2) * FRAMES] = jnp.concatenate(
            [left, right], axis=1
        ).astype(jnp.bfloat16)
    attn_out = (
        lax.dot_general(
            context_ref[...],
            square_ref[CH:, :],
            (((0,), (0,)), ((), ())),
            preferred_element_type=jnp.float32,
        )
        + out_bias
    ).astype(jnp.bfloat16)
    middle_ref[...] = (x + attn_out.astype(jnp.float32)).astype(jnp.bfloat16)


def feed_kernel(middle_ref, vectors_ref, geglu_ref, geglu_bias_ref, down_ref, out_ref, rows_ref):
    pixels = 8
    blocks = 2 * CH // 128
    second_gain, second_shift, down_bias = (
        vectors_ref[FRAMES + i : FRAMES + i + 1, :] for i in range(3, 6)
    )
    middle = middle_ref[...].astype(jnp.float32)
    normed_two = norm_rows(middle, second_gain, second_shift).astype(jnp.bfloat16)
    total = middle + down_bias
    step = 256
    for start in range(0, FF, step):
        lanes = slice(start, start + step)
        gates = slice(FF + start, FF + start + step)
        value = (
            jnp.dot(normed_two, geglu_ref[:, lanes], preferred_element_type=jnp.float32)
            + geglu_bias_ref[:, lanes]
        )
        gate = (
            jnp.dot(normed_two, geglu_ref[:, gates], preferred_element_type=jnp.float32)
            + geglu_bias_ref[:, gates]
        )
        hidden = value * (0.5 * gate * (1.0 + lax.erf(gate * (1.0 / math.sqrt(2.0)))))
        total = total + lax.dot_general(
            hidden.astype(jnp.bfloat16),
            down_ref[:, lanes],
            (((1,), (1,)), ((), ())),
            preferred_element_type=jnp.float32,
        )
    for p in range(pixels):
        near = total[p * FRAMES : p * FRAMES + 32]
        far = total[p * FRAMES + 32 : (p + 1) * FRAMES]
        both = jnp.concatenate([near, far], axis=1)
        for i in range(blocks):
            rows_ref[i, pl.ds(p, 32, stride=pixels), :] = both[:, i * 128 : (i + 1) * 128]
    for i in range(blocks):
        out_ref[:, :, i * 128 : (i + 1) * 128] = (
            rows_ref[i].astype(jnp.bfloat16).reshape(16, 16, 128)
        )


def finish_kernel(x_ref, out_ref):
    received = x_ref[...].astype(jnp.float32)
    for half in range(2):
        lanes = slice(half * CH, (half + 1) * CH)
        for f in range(2):
            rows = received[:, f * 8 : (f + 1) * 8, lanes].reshape(COLS, CH)
            out_ref[half * 2 + f] = rows.T.astype(jnp.bfloat16)


def call(kernel, out_shape, flops, scratch=(), in_specs=None, vmem=8):
    many = isinstance(out_shape, list)
    shapes = [jax.ShapeDtypeStruct(*o) for o in out_shape] if many else out_shape
    spaces = {}
    if in_specs is not None:
        spaces["in_specs"] = [pl.BlockSpec(memory_space=i or pltpu.VMEM) for i in in_specs]
    return pl.pallas_call(
        kernel,
        out_shape=shapes if many else jax.ShapeDtypeStruct(out_shape, jnp.bfloat16),
        scratch_shapes=list(scratch),
        compiler_params=pltpu.CompilerParams(vmem_limit_bytes=vmem * MIB),
        cost_estimate=pl.CostEstimate(flops=flops, bytes_accessed=4 * MIB, transcendentals=0),
        **spaces,
    )


def position_rows():
    frames = np.array([d * 4 + high * 2 + low for high in range(2) for d in range(16) for low in range(2)])
    rates = 10000.0 ** (-2.0 * np.arange(CH // 2) / CH)
    angles = frames[:, None] * rates[None, :]
    return np.stack([np.sin(angles), np.cos(angles)], axis=-1).reshape(FRAMES, CH).astype(np.float32)


def per_device(
    features,
    stale_edges,
    conv_weight,
    conv_bias,
    first_gain,
    first_shift,
    query_weight,
    key_weight,
    value_weight,
    out_weight,
    out_bias,
    second_gain,
    second_shift,
    geglu_weight,
    geglu_bias,
    down_weight,
    down_bias,
):
    frame = ("x", "yh", "c")
    patch = ("yl", "z")
    packed = call(pack_weight_kernel, (16, 3 * TAPS_PAD + PIECE), 10**6)(
        conv_weight.transpose(0, 1, 3, 2)
    )
    mirrored = [(h * 4 + l, (1 - h) * 4 + 3 - l) for h in range(2) for l in range(4)]
    other = lax.ppermute(packed, ("yh", "yl"), mirrored)
    place = jnp.stack([lax.axis_index(a) for a in frame]).astype(jnp.int32)
    upper_half = place[1] == 0
    pair = jnp.stack([jnp.where(upper_half, packed, other), jnp.where(upper_half, other, packed)])
    fanned = jnp.broadcast_to(pair[None], (4,) + pair.shape)
    weight = lax.all_to_all(fanned, "x", 0, 0, tiled=True).reshape(8, 16, 3 * TAPS_PAD + PIECE)

    rims = stale_edges.transpose(0, 1, 3, 2)
    above = lax.ppermute(rims[:, 1], patch, [(i, i + 1) for i in range(PATCHES - 1)])
    below = lax.ppermute(rims[:, 0], patch, [(i + 1, i) for i in range(PATCHES - 1)])

    sides, order = call(
        conv_params_kernel,
        [((8, CH), jnp.float32), ((CH, CH), jnp.bfloat16)],
        10**6,
        in_specs=[None, pltpu.SMEM],
    )(conv_bias[None], place)
    band = features[:, 0].transpose(0, 2, 1)
    upper = call(tokens_kernel, (4 * COLS, 2 * CH), TOKENS_FLOPS)(above, band)
    under = call(tokens_kernel, (4 * COLS, TAPS_PAD - 2 * CH), 12*10**9)(below)
    weight, upper = lax.optimization_barrier((weight, upper))
    theirs = lax.ppermute(weight, "c", [(0, 1), (1, 0)])
    first = call(conv_first_kernel, [((512, CH), jnp.float32)], 10**9, vmem=24)(
        upper, under, weight, sides, order
    )[0]
    outgoing = call(conv_second_kernel, (16, 16, 2 * CH), 10**9, vmem=24)(
        upper, under, theirs, sides, order, first
    )
    owned = lax.all_to_all(outgoing, frame, 0, 0, tiled=True)
    rows = [first_gain, first_shift, out_bias, second_gain, second_shift, down_bias]
    query_weight, outgoing = lax.optimization_barrier((query_weight, outgoing))
    spread, square, vectors = call(
        block_params_kernel,
        [
            ((CH, 1024), jnp.bfloat16),
            ((2 * CH, CH), jnp.bfloat16),
            ((FRAMES + 8, CH), jnp.float32),
        ],
        10**6,
    )(
        query_weight,
        key_weight,
        value_weight,
        out_weight,
        position_rows(),
        *(row[None] for row in rows),
    )
    by_pixel = pltpu.VMEM((5, 256, 128), jnp.float32)
    middle = call(
        attention_kernel,
        (512, CH),
        10**9,
        [by_pixel, pltpu.VMEM((CH, 512), jnp.bfloat16)],
        vmem=24,
    )(owned, spread, square, vectors)
    done = call(feed_kernel, (16, 16, 2 * CH), 10**9, [by_pixel], vmem=24)(
        middle, vectors, geglu_weight, geglu_bias[None], down_weight.T
    )
    returned = lax.all_to_all(done, frame, 0, 0, tiled=True)
    result = call(finish_kernel, (4, CH, COLS), 10**6)(returned)
    return result.transpose(0, 2, 1)[:, None]


def solution(mesh):
    split = Mesh(mesh.devices.reshape(4, 2, 2, 4, 8), ("x", "yh", "c", "yl", "z"))
    frame, patch = ("x", "yh", "c"), ("yl", "z")
    return jax.shard_map(
        per_device,
        mesh=split,
        in_specs=(P(frame, patch), P(frame, patch), P(None, None, None, frame)) + (P(),) * 14,
        out_specs=P(frame, patch),
        check_vma=False,
    )
```

```python
import functools
import math

import jax
import jax.numpy as jnp
import numpy as np
from jax import lax
from jax.experimental import pallas as pl
from jax.experimental.pallas import tpu as pltpu
from jax.sharding import Mesh, PartitionSpec as P

HEADS = 8
CH = 320
FF = 1280
TAPS_IN = 960
TAPS_PAD = 1024
SHARE = 20
PIECE = 768
FRAMES = 64
COLS = 128
PATCHES = 32
TOKENS_FLOPS = 5*10**9
MIB = 1024 * 1024


def pack_weight_kernel(w_ref, out_ref):
    blank = jnp.zeros((SHARE, TAPS_PAD - TAPS_IN), jnp.float32)
    rows = jnp.concatenate(
        [
            part
            for b in range(3)
            for part in [w_ref[a, b].astype(jnp.float32) for a in range(3)] + [blank]
        ],
        axis=1,
    )
    last = jnp.concatenate([rows[16:, q * PIECE : (q + 1) * PIECE] for q in range(4)], axis=0)
    out_ref[...] = jnp.concatenate([rows[:16], last], axis=1).astype(jnp.bfloat16)


def tokens_kernel(*refs):
    *parts, out_ref = refs
    for f in range(4):
        stacked = [part[f] for part in parts]
        blank = out_ref.shape[1] - CH * len(parts)
        if blank:
            stacked.append(jnp.zeros((blank, COLS), jnp.bfloat16))
        out_ref[f * COLS : (f + 1) * COLS, :] = jnp.concatenate(stacked, axis=0).T


def convolve(upper_ref, below_ref, w_ref, bias):
    x = jnp.concatenate([upper_ref[...], below_ref[...]], axis=1)
    tokens = x.shape[0]
    position = lax.broadcasted_iota(jnp.int32, (tokens, 1), 0) % COLS
    split = w_ref[:, :, 3 * TAPS_PAD :].astype(jnp.float32)
    last = jnp.concatenate(
        [
            jnp.concatenate([split[chip, q * 4 : (q + 1) * 4] for chip in range(8)], axis=0)
            for q in range(4)
        ],
        axis=1,
    ).astype(jnp.bfloat16)

    def taps(b):
        cols = slice(b * TAPS_PAD, (b + 1) * TAPS_PAD)
        weight = jnp.concatenate([w_ref[:, :, cols].reshape(-1, TAPS_PAD), last[:, cols]], axis=0)
        return lax.dot_general(
            x, weight, (((1,), (1,)), ((), ())), preferred_element_type=jnp.float32
        )

    left = jnp.where(position == 0, 0.0, pltpu.roll(taps(0), 1, 0))
    right = jnp.where(position == COLS - 1, 0.0, pltpu.roll(taps(2), tokens - 1, 0))
    return taps(1) + left + right + bias


def conv_first_kernel(upper_ref, below_ref, w_ref, bias_ref, order_ref, out_ref):
    rows = convolve(upper_ref, below_ref, w_ref, bias_ref[:1, : CH // 2]).astype(jnp.bfloat16)
    out_ref[...] = jnp.dot(rows, order_ref[: CH // 2, :], preferred_element_type=jnp.float32)


def conv_second_kernel(upper_ref, below_ref, w_ref, bias_ref, order_ref, first_ref, out_ref):
    rows = convolve(upper_ref, below_ref, w_ref, bias_ref[1:2, : CH // 2]).astype(jnp.bfloat16)
    ordered = first_ref[...] + jnp.dot(
        rows, order_ref[CH // 2 :, :], preferred_element_type=jnp.float32
    )
    by_owner = ordered.reshape(2, 2, 16, 8, CH)
    both = jnp.concatenate([by_owner[0], by_owner[1]], axis=-1)
    for k in range(16):
        out_ref[k] = jnp.concatenate([both[0, k], both[1, k]], axis=0).astype(jnp.bfloat16)


def norm_rows(values, gain, shift):
    average = jnp.mean(values, axis=-1, keepdims=True)
    centred = values - average
    variance = jnp.mean(centred * centred, axis=-1, keepdims=True)
    return centred * lax.rsqrt(variance + 1e-05) * gain + shift


def conv_params_kernel(bias_ref, place_ref, sides_ref, order_ref):
    core = place_ref[2]
    bias = bias_ref[...]
    by_core = []
    for i in range(2):
        shares = [bias[:, (chip * 2 + i) * SHARE :][:, :SHARE] for chip in range(8)]
        by_core.append(
            jnp.concatenate([s[:, :16] for s in shares] + [s[:, 16:] for s in shares], axis=1)
        )
    sides_ref[:1, : CH // 2] = jnp.where(core == 0, by_core[0], by_core[1])
    sides_ref[1:2, : CH // 2] = jnp.where(core == 0, by_core[1], by_core[0])
    row = lax.broadcasted_iota(jnp.int32, (CH, CH), 0)
    owner = jnp.where(row < CH // 2, core, 1 - core)
    row = jnp.where(row < CH // 2, row, row - CH // 2)
    chip = jnp.where(row < 128, row >> 4, (row - 128) >> 2)
    share = jnp.where(row < 128, row & 15, 16 + (row & 3))
    channel = (chip * 2 + owner) * SHARE + share
    here = channel == lax.broadcasted_iota(jnp.int32, (CH, CH), 1)
    order_ref[...] = jnp.where(here, 1.0, 0.0).astype(jnp.bfloat16)


def block_params_kernel(*refs):
    query, key, value, out = refs[:4]
    rows = refs[4:11]
    spread_ref, square_ref, vectors_ref = refs[11:]
    source = lax.broadcasted_iota(jnp.int32, (CH, 512), 0)
    lane = lax.broadcasted_iota(jnp.int32, (CH, 512), 1)
    there = ((lane & 63) < 40) & (source == (lane >> 6) * 40 + (lane & 63))
    spread = jnp.where(there, 1.0, 0.0).astype(jnp.bfloat16)
    for i, part in enumerate((query, key)):
        spread_ref[:, i * 512 : (i + 1) * 512] = jnp.dot(
            part[...], spread, preferred_element_type=jnp.float32
        ).astype(jnp.bfloat16)
    square_ref[:CH, :] = value[...].astype(jnp.float32).T.astype(jnp.bfloat16)
    square_ref[CH:, :] = out[...]
    vectors_ref[:FRAMES, :] = rows[0][...]
    for i, row in enumerate(rows[1:]):
        vectors_ref[FRAMES + i : FRAMES + i + 1, :] = row[...]
    vectors_ref[FRAMES + 6 :, :] = jnp.zeros((2, CH), jnp.float32)


def attention_kernel(x_ref, spread_ref, square_ref, vectors_ref, middle_ref, rows_ref, context_ref):
    first_gain, first_shift, out_bias = (
        vectors_ref[FRAMES + i : FRAMES + i + 1, :] for i in range(3)
    )
    pixels = 8
    blocks = 2 * CH // 128
    received = x_ref[...].astype(jnp.float32).reshape(256, 2 * CH)
    for i in range(blocks):
        rows_ref[i] = received[:, i * 128 : (i + 1) * 128]
    pieces = []
    for p in range(pixels):
        both = jnp.concatenate(
            [rows_ref[i, pl.ds(p, 32, stride=pixels), :] for i in range(blocks)], axis=1
        )
        pieces += [both[:, :CH], both[:, CH:]]
    x = jnp.concatenate(pieces, axis=0)
    position = vectors_ref[:FRAMES, :]
    normed = norm_rows(x, first_gain, first_shift).reshape(pixels, FRAMES, CH)
    normed = (normed + position[None]).reshape(pixels * FRAMES, CH).astype(jnp.bfloat16)

    queries, key_rows = (
        jnp.dot(
            normed, spread_ref[:, i * 512 : (i + 1) * 512], preferred_element_type=jnp.float32
        ).astype(jnp.bfloat16)
        for i in range(2)
    )
    across = (((1,), (1,)), ((), ()))
    values = lax.dot_general(
        square_ref[:CH, :], normed, across, preferred_element_type=jnp.float32
    ).astype(jnp.bfloat16)
    scale = 1.0 / math.sqrt(CH // HEADS)
    head_of = lax.broadcasted_iota(jnp.int32, (1, 256), 1) >> 6
    units = [(p, quad) for p in range(pixels) for quad in range(2)]
    scores = []
    for p, quad in units:
        rows = slice(p * FRAMES, (p + 1) * FRAMES)
        lanes = slice(quad * 256, (quad + 1) * 256)
        query = queries[rows, lanes]
        stacked = jnp.concatenate(
            [jnp.where(head_of == h, query, jnp.zeros_like(query)) for h in range(4)], axis=0
        )
        scores.append(
            lax.dot_general(
                key_rows[rows, lanes], stacked, across, preferred_element_type=jnp.float32
            )
        )
    scores = jnp.concatenate(scores, axis=1)
    expo = jnp.exp((scores - jnp.max(scores, axis=0, keepdims=True)) * scale)
    probs = (expo * (1.0 / jnp.sum(expo, axis=0, keepdims=True))).astype(jnp.bfloat16)
    contexts = []
    for i, (p, quad) in enumerate(units):
        rows = slice(p * FRAMES, (p + 1) * FRAMES)
        mixed = jnp.dot(
            values[quad * 160 : (quad + 1) * 160, rows],
            probs[:, i * 256 : (i + 1) * 256],
            preferred_element_type=jnp.float32,
        )
        for h in range(4):
            contexts.append(mixed[h * 40 : (h + 1) * 40, h * FRAMES : (h + 1) * FRAMES])
    for p in range(0, pixels, 2):
        left = jnp.concatenate(contexts[p * HEADS : (p + 1) * HEADS], axis=0)
        right = jnp.concatenate(contexts[(p + 1) * HEADS : (p + 2) * HEADS], axis=0)
        context_ref[:, p * FRAMES : (p + 2) * FRAMES] = jnp.concatenate(
            [left, right], axis=1
        ).astype(jnp.bfloat16)
    attn_out = (
        lax.dot_general(
            context_ref[...],
            square_ref[CH:, :],
            (((0,), (0,)), ((), ())),
            preferred_element_type=jnp.float32,
        )
        + out_bias
    ).astype(jnp.bfloat16)
    middle_ref[...] = (x + attn_out.astype(jnp.float32)).astype(jnp.bfloat16)


def feed_kernel(middle_ref, vectors_ref, geglu_ref, geglu_bias_ref, down_ref, out_ref, rows_ref):
    pixels = 8
    blocks = 2 * CH // 128
    second_gain, second_shift, down_bias = (
        vectors_ref[FRAMES + i : FRAMES + i + 1, :] for i in range(3, 6)
    )
    middle = middle_ref[...].astype(jnp.float32)
    normed_two = norm_rows(middle, second_gain, second_shift).astype(jnp.bfloat16)
    total = middle + down_bias
    step = 256
    pieces = []
    for start in range(0, FF, step):
        lanes = slice(start, start + step)
        gates = slice(FF + start, FF + start + step)
        value = (
            jnp.dot(normed_two, geglu_ref[:, lanes], preferred_element_type=jnp.float32)
            + geglu_bias_ref[:, lanes]
        )
        gate = (
            jnp.dot(normed_two, geglu_ref[:, gates], preferred_element_type=jnp.float32)
            + geglu_bias_ref[:, gates]
        )
        hidden = value * (0.5 * gate * (1.0 + lax.erf(gate * (1.0 / math.sqrt(2.0)))))
        pieces.append(hidden.astype(jnp.bfloat16))
    total = total + lax.dot_general(
        jnp.concatenate(pieces, axis=1),
        down_ref[...],
        (((1,), (1,)), ((), ())),
        preferred_element_type=jnp.float32,
    )
    for p in range(pixels):
        near = total[p * FRAMES : p * FRAMES + 32]
        far = total[p * FRAMES + 32 : (p + 1) * FRAMES]
        both = jnp.concatenate([near, far], axis=1)
        for i in range(blocks):
            rows_ref[i, pl.ds(p, 32, stride=pixels), :] = both[:, i * 128 : (i + 1) * 128]
    for i in range(blocks):
        out_ref[:, :, i * 128 : (i + 1) * 128] = (
            rows_ref[i].astype(jnp.bfloat16).reshape(16, 16, 128)
        )


def finish_kernel(x_ref, out_ref):
    received = x_ref[...].astype(jnp.float32)
    for half in range(2):
        lanes = slice(half * CH, (half + 1) * CH)
        for f in range(2):
            rows = received[:, f * 8 : (f + 1) * 8, lanes].reshape(COLS, CH)
            out_ref[half * 2 + f] = rows.T.astype(jnp.bfloat16)


def call(kernel, out_shape, flops, scratch=(), in_specs=None, vmem=8):
    many = isinstance(out_shape, list)
    shapes = [jax.ShapeDtypeStruct(*o) for o in out_shape] if many else out_shape
    spaces = {}
    if in_specs is not None:
        spaces["in_specs"] = [pl.BlockSpec(memory_space=i or pltpu.VMEM) for i in in_specs]
    return pl.pallas_call(
        kernel,
        out_shape=shapes if many else jax.ShapeDtypeStruct(out_shape, jnp.bfloat16),
        scratch_shapes=list(scratch),
        compiler_params=pltpu.CompilerParams(vmem_limit_bytes=vmem * MIB),
        cost_estimate=pl.CostEstimate(flops=flops, bytes_accessed=4 * MIB, transcendentals=0),
        **spaces,
    )


def position_rows():
    frames = np.array([d * 4 + high * 2 + low for high in range(2) for d in range(16) for low in range(2)])
    rates = 10000.0 ** (-2.0 * np.arange(CH // 2) / CH)
    angles = frames[:, None] * rates[None, :]
    return np.stack([np.sin(angles), np.cos(angles)], axis=-1).reshape(FRAMES, CH).astype(np.float32)


def per_device(
    features,
    stale_edges,
    conv_weight,
    conv_bias,
    first_gain,
    first_shift,
    query_weight,
    key_weight,
    value_weight,
    out_weight,
    out_bias,
    second_gain,
    second_shift,
    geglu_weight,
    geglu_bias,
    down_weight,
    down_bias,
):
    frame = ("x", "yh", "c")
    patch = ("yl", "z")
    packed = call(pack_weight_kernel, (16, 3 * TAPS_PAD + PIECE), 10**6)(
        conv_weight.transpose(0, 1, 3, 2)
    )
    mirrored = [(h * 4 + l, (1 - h) * 4 + 3 - l) for h in range(2) for l in range(4)]
    other = lax.ppermute(packed, ("yh", "yl"), mirrored)
    place = jnp.stack([lax.axis_index(a) for a in frame]).astype(jnp.int32)
    upper_half = place[1] == 0
    pair = jnp.stack([jnp.where(upper_half, packed, other), jnp.where(upper_half, other, packed)])
    fanned = jnp.broadcast_to(pair[None], (4,) + pair.shape)
    weight = lax.all_to_all(fanned, "x", 0, 0, tiled=True).reshape(8, 16, 3 * TAPS_PAD + PIECE)

    rims = stale_edges.transpose(0, 1, 3, 2)
    above = lax.ppermute(rims[:, 1], patch, [(i, i + 1) for i in range(PATCHES - 1)])
    below = lax.ppermute(rims[:, 0], patch, [(i + 1, i) for i in range(PATCHES - 1)])

    sides, order = call(
        conv_params_kernel,
        [((8, CH), jnp.float32), ((CH, CH), jnp.bfloat16)],
        10**6,
        in_specs=[None, pltpu.SMEM],
    )(conv_bias[None], place)
    band = features[:, 0].transpose(0, 2, 1)
    upper = call(tokens_kernel, (4 * COLS, 2 * CH), TOKENS_FLOPS)(above, band)
    under = call(tokens_kernel, (4 * COLS, TAPS_PAD - 2 * CH), 12*10**9)(below)
    weight, upper = lax.optimization_barrier((weight, upper))
    theirs = lax.ppermute(weight, "c", [(0, 1), (1, 0)])
    first = call(conv_first_kernel, [((512, CH), jnp.float32)], 10**9, vmem=24)(
        upper, under, weight, sides, order
    )[0]
    outgoing = call(conv_second_kernel, (16, 16, 2 * CH), 10**9, vmem=24)(
        upper, under, theirs, sides, order, first
    )
    owned = lax.all_to_all(outgoing, frame, 0, 0, tiled=True)
    rows = [first_gain, first_shift, out_bias, second_gain, second_shift, down_bias]
    query_weight, outgoing = lax.optimization_barrier((query_weight, outgoing))
    spread, square, vectors = call(
        block_params_kernel,
        [
            ((CH, 1024), jnp.bfloat16),
            ((2 * CH, CH), jnp.bfloat16),
            ((FRAMES + 8, CH), jnp.float32),
        ],
        10**6,
    )(
        query_weight,
        key_weight,
        value_weight,
        out_weight,
        position_rows(),
        *(row[None] for row in rows),
    )
    by_pixel = pltpu.VMEM((5, 256, 128), jnp.float32)
    middle = call(
        attention_kernel,
        (512, CH),
        10**9,
        [by_pixel, pltpu.VMEM((CH, 512), jnp.bfloat16)],
        vmem=24,
    )(owned, spread, square, vectors)
    done = call(feed_kernel, (16, 16, 2 * CH), 10**9, [by_pixel], vmem=24)(
        middle, vectors, geglu_weight, geglu_bias[None], down_weight.T
    )
    returned = lax.all_to_all(done, frame, 0, 0, tiled=True)
    result = call(finish_kernel, (4, CH, COLS), 10**6)(returned)
    return result.transpose(0, 2, 1)[:, None]


def solution(mesh):
    split = Mesh(mesh.devices.reshape(4, 2, 2, 4, 8), ("x", "yh", "c", "yl", "z"))
    frame, patch = ("x", "yh", "c"), ("yl", "z")
    return jax.shard_map(
        per_device,
        mesh=split,
        in_specs=(P(frame, patch), P(frame, patch), P(None, None, None, frame)) + (P(),) * 14,
        out_specs=P(frame, patch),
        check_vma=False,
    )
```
